256 devices in a mesh: ctx: 32 (over z, x_lo, core), tp: 8 (over x_hi, y).
Axes of the slice: x: 4 (x_hi: 2, x_lo: 2; x = x_hi * 2 + x_lo), y: 4, z: 8, core: 2. Of those that a mesh axis runs over, the one named last changes fastest.
Arguments:
- normed_rows: bfloat16 [4096, 5120], P('ctx', 'tp'), may hold values from -6 to 6
- query_rows: bfloat16 [4096, 3072], P('ctx', 'tp'), may hold values from -5 to 5
- key_rows: bfloat16 [4096, 3072], P('ctx', 'tp'), may hold values from -5 to 5
- value_rows: bfloat16 [4096, 3072], P('ctx', 'tp'), may hold values from -6 to 6
- grad_output: bfloat16 [4096, 3072], P('ctx', 'tp'), may hold values from -6 to 6
- stretch_ids: int32 [16], replicated, may hold values from 0 to 7, never falling along the last dimension, each value on 1 to 4 neighbouring positions
Outputs:
- query_grad: bfloat16 [5120, 3072], P('ctx', 'tp')
- key_grad: bfloat16 [5120, 3072], P('ctx', 'tp')
- value_grad: bfloat16 [5120, 3072], P('ctx', 'tp')
The draws below stay inside these ranges and needn't reach their ends.
Inputs may be any that keep to these rules, and one draw needn't show every extreme that they name: `stretch_ids`: never falls from block to block; each stretch spans 1 to 4 consecutive blocks of 256 tokens, and some stretch exactly 4; every number of the range is used.
All inputs are finite; a program needn't handle non-finite values.
Results may differ from the reference program's by a relative error of at most 0.0075.
Values may be sent and summed in bfloat16 or wider, within the bound.
No kernel may reach another device: no remote copies, remote signals or barrier semaphores. Data moves between devices by JAX's collectives and lax.ppermute only.
A program may use at most 128 MiB of HBM per device.

```python
import math
import jax
import jax.numpy as jnp
import numpy as np
from jax import lax

D = 5120
HEADS = 24
HD = 128
BLOCK = 256
TOKENS = 4096
NB = 16


def draw_query_rows(key, part):
    key = jax.random.fold_in(key, 11)
    drawn_rows = jnp.clip(jax.random.normal(key, (TOKENS, HEADS * HD), jnp.float32), -5.0, 5.0)
    return drawn_rows.astype(jnp.bfloat16)


def draw_key_rows(key, part):
    key = jax.random.fold_in(key, 23)
    drawn_rows = jnp.clip(jax.random.normal(key, (TOKENS, HEADS * HD), jnp.float32), -5.0, 5.0)
    return drawn_rows.astype(jnp.bfloat16)


def spiked(entries, key, source, target, parts, factor):
    def block_of(position):
        return (jnp.arange(entries.shape[position]) // (entries.shape[position] // parts)).reshape((-1,) + (1,) * (entries.ndim - 1 - position))

    first = jax.random.permutation(key, parts)[block_of(target)]
    far = (block_of(target) + parts // 2) % parts
    return jnp.where((block_of(source) == first) | (block_of(source) == far), factor * entries, entries)


def level_of(rng, extent, pieces, least, largest):
    loudness, own = 1.0, jax.random.fold_in(rng, 6)
    for axis_at, parts in pieces:
        steps = jnp.exp(jax.random.uniform(jax.random.fold_in(own, axis_at), (parts,), jnp.float32, least / len(pieces), largest / len(pieces)))
        loudness = loudness * jnp.repeat(steps, extent[axis_at] // parts).reshape([-1 if axis == axis_at else 1 for axis in range(len(extent))])
    return loudness


def split_up(number_of, total, limit, skew):
    weights = [(1 << 20) // math.isqrt(rank ** skew) + 1 for rank in range(2, number_of + 1)]
    surplus, holding = total - limit - (number_of - 1), [1] * (number_of - 1)
    while surplus > 0:
        candidates = [i for i in range(number_of - 1) if holding[i] < limit]
        whole, left = sum([weights[i] for i in candidates]), surplus
        for i in candidates:
            more = min(limit - holding[i], max(1, left * weights[i] // whole), surplus)
            holding[i] = holding[i] + more
            surplus = surplus - more
    return np.array([limit] + holding)


def uneven_parts(rng, number_of, total, bound, slope):
    if number_of == 2:
        one = jax.random.randint(rng, (), max(1, total - bound), min(bound, total - 1) + 1)
        return jnp.stack([one, total - one])
    lengths = jnp.asarray(split_up(number_of, total, bound, slope), jnp.int32)
    pairs = (number_of - 1) // 2
    source_of, receiver = lengths[1:1 + 2 * pairs:2], lengths[2:2 + 2 * pairs:2]
    margin = jnp.minimum(source_of - 1, bound - receiver)
    shifted = jax.random.randint(jax.random.fold_in(rng, 1), (pairs,), 0, 1 << 20) % (margin + 1)
    lengths = lengths.at[1:1 + 2 * pairs:2].set(source_of - shifted).at[2:2 + 2 * pairs:2].set(receiver + shifted)
    return lengths[jax.random.permutation(jax.random.fold_in(rng, 2), number_of)]


def centred(key, shape, width, most, shards=(), kind=jnp.bfloat16):
    gain = level_of(key, shape, shards, -0.22, 0.18) if shards else 1.0
    result = jax.random.normal(key, shape, jnp.float32) * width * gain
    return jnp.minimum(jnp.maximum(result, -most), most).astype(kind)


def bell_draw_with(rng, shape, scale, bound, split, heavy, kind=jnp.bfloat16):
    values = scale * jax.random.normal(rng, shape, jnp.float32)
    if split:
        values = values * level_of(rng, shape, split, -0.22, 0.18)
    return jnp.clip(spiked(values, jax.random.fold_in(rng, 3), *heavy), -bound, bound).astype(kind)


def setup_inputs(seed: int = 0) -> dict:
    key_list = jax.random.split(jax.random.key(seed), 7)
    normed_rows = bell_draw_with(key_list[0], (TOKENS, D), 1.0, 6.0, ((0, 32), (1, 8)), (0, 1, 32, 2.75))
    query_rows = draw_query_rows(jax.random.fold_in(key_list[6], 71), 0)
    key_rows = draw_key_rows(jax.random.fold_in(key_list[6], 71), 0)
    value_rows = centred(key_list[3], (TOKENS, HEADS * HD), 1.0, 6.0, ((0, 32), (1, 8)))
    grad_output = centred(key_list[4], (TOKENS, HEADS * HD), 1.0, 6.0, ((0, 32), (1, 8)))
    stretch_ids = jnp.searchsorted(jnp.cumsum(uneven_parts(key_list[5], NB // 2, NB, 4, 1)), jnp.arange(NB), side="right").astype(jnp.int32)
    return {"normed_rows": normed_rows, "query_rows": query_rows, "key_rows": key_rows, "value_rows": value_rows, "grad_output": grad_output, "stretch_ids": stretch_ids}


def token_stretches(stretch_ids, length, offset):
    blocks = (offset + jnp.arange(length, dtype=jnp.int32)) // BLOCK
    table = jnp.arange(stretch_ids.shape[0], dtype=jnp.int32)
    return jnp.sum(jnp.where(blocks[:, None] == table[None, :], stretch_ids[None, :], 0), axis=1)


def to_half(values):
    return lax.optimization_barrier(values.astype(jnp.bfloat16)).astype(jnp.float32)


def reference(normed_rows, query_rows, key_rows, value_rows, grad_output, stretch_ids):
    factor = HD ** -0.5
    stretches = token_stretches(stretch_ids, TOKENS, 0)
    allowed = stretches[:, None] >= stretches[None, :]

    def split_heads(rows):
        return rows.astype(jnp.float32).reshape(TOKENS, HEADS, HD).transpose(1, 0, 2)

    def per_head(inputs):
        query_one, key_one, value_one, grad_one = inputs
        scores = jnp.einsum('qd,kd->qk', query_one, key_one) * factor
        row_max = jnp.max(jnp.where(allowed, scores, -jnp.inf), axis=1, keepdims=True)
        row_total = jnp.sum(jnp.where(allowed, jnp.exp(scores - row_max), 0.0), axis=1, keepdims=True)
        log_sum = row_max + jnp.log(row_total)
        attn_prob = jnp.where(allowed, jnp.exp(scores - log_sum), 0.0)
        grad_prob = jnp.einsum('qd,kd->qk', grad_one, value_one)
        row_delta = jnp.sum(attn_prob * grad_prob, axis=1, keepdims=True)
        dscore = to_half(factor * attn_prob * (grad_prob - row_delta))
        prob_half = to_half(attn_prob)
        dquery = jnp.einsum('qk,kd->qd', dscore, key_one)
        key_grad_rows = jnp.einsum('qk,qd->kd', dscore, query_one)
        value_grad_rows = jnp.einsum('qk,qd->kd', prob_half, grad_one)
        return dquery, key_grad_rows, value_grad_rows

    heads_out = lax.map(per_head, (split_heads(query_rows), split_heads(key_rows),
                                   split_heads(value_rows), split_heads(grad_output)))

    def join_heads(values):
        return values.transpose(1, 0, 2).reshape(TOKENS, HEADS * HD).astype(jnp.bfloat16)

    results = []
    for values in heads_out:
        rows_g = join_heads(values)
        total = jnp.dot(normed_rows.T, rows_g, preferred_element_type=jnp.float32)
        results.append(total.astype(jnp.bfloat16))
    return (results[0], results[1], results[2])
```

```python
import functools
import math

import jax
import jax.numpy as jnp
from jax import lax
from jax.experimental import pallas as pl
from jax.experimental.pallas import tpu as pltpu
from jax.sharding import PartitionSpec as P

HD = 128
HEADS_DEV = 3
W = HD * HEADS_DEV
ROWS = 128
PLANES = 8
FACTOR = HD ** (-0.5)
SCALE2 = FACTOR * math.log2(math.e)
LOW = -1e30
F32 = jnp.float32
BF16 = jnp.bfloat16

CTX = 32
CORE_SWAP = [(i, i ^ 1) for i in range(CTX)]
X_SWAP = [(i, i ^ 2) for i in range(CTX)]
DIAG_SWAP = [(i, i ^ 3) for i in range(CTX)]
Z_UP = [(i, (i + 4) % CTX) for i in range(CTX)]
Z_DOWN = [(i, (i - 4) % CTX) for i in range(CTX)]
Z_GROUPS = [[4 * z + j for z in range(PLANES)] for j in range(4)]
TRANSPOSE = [
    ((4 * z + j) * 8 + t, (4 * t + j) * 8 + z)
    for z in range(8)
    for j in range(4)
    for t in range(8)
]
TP_X = [(t, t ^ 4) for t in range(8)]
TP_UP = [(t, (t // 4) * 4 + (t + 1) % 4) for t in range(8)]
TP_DOWN = [(t, (t // 4) * 4 + (t + 3) % 4) for t in range(8)]

NT = (((1,), (1,)), ((), ()))
TN = (((0,), (0,)), ((), ()))
NN = (((1,), (0,)), ((), ()))


def dot(a, b, dims):
    return lax.dot_general(a, b, dims, preferred_element_type=F32)


def ring(part):
    half = part.shape[0] // 2
    up, down = [part], [part]
    for _ in range(3):
        up.append(lax.ppermute(up[-1], "ctx", Z_UP))
        down.append(lax.ppermute(down[-1], "ctx", Z_DOWN))
    far_a = lax.ppermute(up[3][:half], "ctx", Z_UP)
    far_b = lax.ppermute(down[3][half:], "ctx", Z_DOWN)
    return [part, up[1], down[1], up[2], down[2], up[3], down[3], far_a, far_b]


RING_SHIFT = (0, -1, 1, -2, 2, -3, 3, 4)


def fill(scratch, refs, columns=None):
    at = 0
    for ref in refs:
        n = ref.shape[0]
        scratch[at : at + n, :] = ref[...] if columns is None else ref[:, columns]
        at += n


def lane_row(values, width=ROWS):
    return jnp.concatenate([jnp.full((1, width), v, jnp.int32) for v in values], axis=1)


def fold(x, op):
    y = x.reshape(x.shape[0] // 8, 8, x.shape[1])
    return op(y, axis=0)


def plane_tables(place, ids):
    z, xl = place[0], place[1]
    own = ids[2 * z + xl]
    other = ids[2 * z + 1 - xl]
    return [own, own, other, other]


def ring_tables(place, ids):
    z, xl = place[0], place[1]
    return [ids[2 * lax.rem(z + s + PLANES, PLANES) + xl] for s in RING_SHIFT]


def stats_kernel(place, ids, *refs):
    qg, k_in, v_in, out = refs[:4], refs[4:13], refs[13:22], refs[22]
    qc, kc, vc, sc = refs[23:]
    fill(qc, qg)
    fill(kc, k_in)
    fill(vc, v_in)
    q_row = lane_row(plane_tables(place, ids))
    k_st = ring_tables(place, ids)
    out[...] = jnp.zeros_like(out)
    for h in range(HEADS_DEV):
        cols = slice(h * HD, (h + 1) * HD)
        gcols = slice(W + h * HD, W + (h + 1) * HD)
        qh = qc[:, cols]
        gh = qc[:, gcols]
        top = jnp.full((8, 4 * ROWS), LOW, F32)
        for k in range(PLANES):
            rows = slice(k * ROWS, (k + 1) * ROWS)
            s = dot(kc[rows, cols], qh, NT) * SCALE2
            s = jnp.where(q_row >= k_st[k], s, LOW)
            sc[rows, :] = s
            top = jnp.maximum(top, fold(s, jnp.max))
        m = jnp.maximum(jnp.max(top, axis=0, keepdims=True), 0.1 * LOW)
        total = jnp.zeros((8, 4 * ROWS), F32)
        weighted = jnp.zeros((8, 4 * ROWS), F32)
        for k in range(PLANES):
            rows = slice(k * ROWS, (k + 1) * ROWS)
            dp = dot(vc[rows, cols], gh, NT)
            e = jnp.exp2(sc[rows, :] - m)
            total = total + fold(e, jnp.sum)
            weighted = weighted + fold(e * dp, jnp.sum)
        out[h : h + 1, :] = m
        out[3 + h : 4 + h, :] = jnp.sum(total, axis=0, keepdims=True)
        out[6 + h : 7 + h, :] = jnp.sum(weighted, axis=0, keepdims=True)


def combine_kernel(s0, s1, s2, s3, out, own):
    parts = []
    for d, ref in enumerate((s0, s1, s2, s3)):
        full = ref[...]
        parts.append(
            jnp.concatenate(
                [full[:, (r ^ d) * ROWS : ((r ^ d) + 1) * ROWS] for r in range(4)], axis=1
            )
        )
    m = [p[0:3] for p in parts]
    top = jnp.maximum(jnp.maximum(m[0], m[1]), jnp.maximum(m[2], m[3]))
    total = jnp.zeros_like(top)
    weighted = jnp.zeros_like(top)
    for p in parts:
        w = jnp.exp2(p[0:3] - top)
        total = total + w * p[3:6]
        weighted = weighted + w * p[6:9]
    lse = top + jnp.log2(total)
    delta = weighted / total
    res = jnp.concatenate([lse, delta, jnp.zeros((2, 4 * ROWS), F32)], axis=0)
    out[...] = res
    for i in range(PLANES):
        own[i * 8 : (i + 1) * 8, :] = res[:, :ROWS]


def dquery_kernel(place, ids, *refs):
    qg, k_in, v_in, lsd = refs[:4], refs[4:13], refs[13:22], refs[22]
    keep, send = refs[23:25]
    qc, kc, vc, ds = refs[25:]
    fill(qc, qg)
    fill(kc, k_in)
    fill(vc, v_in)
    q_row = lane_row(plane_tables(place, ids))
    k_st = ring_tables(place, ids)
    for h in range(HEADS_DEV):
        cols = slice(h * HD, (h + 1) * HD)
        gcols = slice(W + h * HD, W + (h + 1) * HD)
        qh = qc[:, cols]
        gh = qc[:, gcols]
        lse = lsd[h : h + 1, :]
        delta = lsd[3 + h : 4 + h, :]
        for k in range(PLANES):
            rows = slice(k * ROWS, (k + 1) * ROWS)
            s = dot(kc[rows, cols], qh, NT) * SCALE2
            p = jnp.where(q_row >= k_st[k], jnp.exp2(s - lse), 0.0)
            dp = dot(vc[rows, cols], gh, NT)
            ds[rows, :] = (FACTOR * p * (dp - delta)).astype(BF16)
        dq = dot(kc[:, cols], ds[...], TN).T
        for r in range(4):
            piece = dq[r * ROWS : (r + 1) * ROWS, :]
            if r % 2 == 0:
                keep[r // 2, :, cols] = piece
            else:
                send[r // 2, :, cols] = piece.astype(BF16)


def dkey_kernel(place, ids, *refs):
    kv, qg, stats = refs[:4], refs[4], refs[5]
    keep, send = refs[6:]
    z, xl = place[0], place[1]
    q_row = lane_row([ids[2 * i + xl] for i in range(PLANES)])
    k_st = plane_tables(place, ids)
    for h in range(HEADS_DEV):
        cols = slice(h * HD, (h + 1) * HD)
        vcols = slice(W + h * HD, W + (h + 1) * HD)
        qh = qg[:, cols]
        gh = qg[:, vcols]
        lse = jnp.concatenate([stats[8 * i + h : 8 * i + h + 1, :] for i in range(PLANES)], axis=1)
        delta = jnp.concatenate(
            [stats[8 * i + 3 + h : 8 * i + 4 + h, :] for i in range(PLANES)], axis=1
        )
        for r in range(4):
            s = dot(kv[r][:, cols], qh, NT) * SCALE2
            p = jnp.where(q_row >= k_st[r], jnp.exp2(s - lse), 0.0)
            dp = dot(kv[r][:, vcols], gh, NT)
            ds = (FACTOR * p * (dp - delta)).astype(BF16)
            dv = dot(p.astype(BF16), gh, NN)
            dk = dot(ds, qh, NN)
            if r % 2 == 0:
                keep[r // 2, :, cols] = dk
                keep[r // 2, :, vcols] = dv
            else:
                send[r // 2, :, cols] = dk.astype(BF16)
                send[r // 2, :, vcols] = dv.astype(BF16)


def normed_kernel(place, pair, up, down, up2, down2, out):
    t = place[3]
    y = lax.rem(t, 4)
    xh = lax.div(t, 4)

    def put(block, hi, yy):
        at = pl.multiple_of((hi * 4 + lax.rem(yy + 4, 4)) * ROWS, ROWS)
        out[:, pl.ds(at, ROWS)] = block.T

    for ref, dy in ((pair, 0), (up, -1), (down, 1)):
        put(ref[:ROWS, :], xh, y + dy)
        put(ref[ROWS:, :], 1 - xh, y + dy)
    put(up2[...], xh, y - 2)
    put(down2[...], 1 - xh, y + 2)


def product(place, at, b, keep, send):
    core = place[2]
    for half in range(2):
        mine = pl.multiple_of((2 * half + core) * 160, 160)
        theirs = pl.multiple_of((2 * half + 1 - core) * 160, 160)
        keep[half, :, :] = dot(at[pl.ds(mine, 160), :], b[...], NN)
        send[half, :, :] = dot(at[pl.ds(theirs, 160), :], b[...], NN).astype(BF16)


def product_ring_kernel(place, at, *refs):
    blocks, keep, send, b = refs[:9], refs[9], refs[10], refs[11]
    z = place[0]
    for ref, s in zip(blocks[:7], RING_SHIFT):
        b[pl.ds(pl.multiple_of(lax.rem(z + s + PLANES, PLANES) * ROWS, ROWS), ROWS), :] = ref[...]
    far = pl.multiple_of(lax.rem(z + 4, PLANES) * ROWS, ROWS)
    b[pl.ds(far, ROWS), :] = jnp.concatenate([blocks[7][...], blocks[8][...]], axis=0)
    product(place, at, b, keep, send)


def call(kernel, out_shape, *args, scratch=(), smem=0, flops=0, name=None):
    specs = [pl.BlockSpec(memory_space=pltpu.SMEM)] * smem
    specs += [pl.BlockSpec(memory_space=pltpu.VMEM)] * (len(args) - smem)
    size = sum(math.prod(a.shape) * a.dtype.itemsize for a in args)
    return pl.pallas_call(
        kernel,
        out_shape=out_shape,
        in_specs=specs,
        out_specs=jax.tree.map(lambda _: pl.BlockSpec(memory_space=pltpu.VMEM), out_shape),
        scratch_shapes=list(scratch),
        compiler_params=pltpu.CompilerParams(vmem_limit_bytes=40 * 2**20),
        cost_estimate=pl.CostEstimate(flops=flops, bytes_accessed=size, transcendentals=0),
        name=name,
    )(*args)


def shaped(shape, dtype):
    return jax.ShapeDtypeStruct(shape, dtype)


def plane_gather(part):
    across = lax.ppermute(part, "ctx", X_SWAP)
    beside = lax.ppermute(part, "ctx", CORE_SWAP)
    diag = lax.ppermute(across, "ctx", CORE_SWAP)
    return [part, beside, across, diag]


def plane_sum(keep, send):
    got = lax.ppermute(send, "ctx", CORE_SWAP).astype(F32)
    mine = keep[0] + got[0]
    other = (keep[1] + got[1]).astype(BF16)
    return mine + lax.ppermute(other, "ctx", X_SWAP).astype(F32)


def row_sum(keep, send, xl):
    got = lax.ppermute(send, "ctx", CORE_SWAP).astype(F32)
    both = keep + got
    mine = lax.dynamic_index_in_dim(both, xl, 0, keepdims=False)
    other = lax.dynamic_index_in_dim(both, 1 - xl, 0, keepdims=False).astype(BF16)
    return mine + lax.ppermute(other, "ctx", X_SWAP).astype(F32)


def shards(normed_rows, query_rows, key_rows, value_rows, grad_output, stretch_ids):
    ctx = lax.axis_index("ctx")
    xl = lax.rem(lax.div(ctx, 2), 2)
    place = jnp.stack([lax.div(ctx, 4), xl, lax.rem(ctx, 2), lax.axis_index("tp")]).astype(
        jnp.int32
    )
    qg_own = jnp.concatenate([query_rows, grad_output], axis=1)
    kv_own = jnp.concatenate([key_rows, value_rows], axis=1)

    key_ring = ring(key_rows)
    value_ring = ring(value_rows)
    qg_all = lax.all_gather(qg_own, "ctx", axis=0, tiled=True, axis_index_groups=Z_GROUPS)
    qg_plane = plane_gather(qg_own)

    wide = [
        pltpu.VMEM((4 * ROWS, 2 * W), BF16),
        pltpu.VMEM((PLANES * ROWS, W), BF16),
        pltpu.VMEM((PLANES * ROWS, W), BF16),
    ]
    stats = call(
        stats_kernel,
        shaped((16, 4 * ROWS), F32),
        place,
        stretch_ids,
        *qg_plane,
        *key_ring,
        *value_ring,
        smem=2,
        scratch=wide + [pltpu.VMEM((PLANES * ROWS, 4 * ROWS), F32)],
        flops=2 * 2 * 1024 * 512 * W,
        name="softmax_statistics",
    )
    lsd, own_stats = call(
        combine_kernel,
        (shaped((8, 4 * ROWS), F32), shaped((8 * PLANES, ROWS), F32)),
        stats,
        lax.ppermute(stats, "ctx", CORE_SWAP),
        lax.ppermute(stats, "ctx", X_SWAP),
        lax.ppermute(stats, "ctx", DIAG_SWAP),
        name="combine_statistics",
    )
    all_stats = lax.all_to_all(
        own_stats, "ctx", split_axis=0, concat_axis=0, tiled=True, axis_index_groups=Z_GROUPS
    )
    dq_keep, dq_send = call(
        dquery_kernel,
        (shaped((2, ROWS, W), F32), shaped((2, ROWS, W), BF16)),
        place,
        stretch_ids,
        *qg_plane,
        *key_ring,
        *value_ring,
        lsd,
        smem=2,
        scratch=wide + [pltpu.VMEM((PLANES * ROWS, 4 * ROWS), BF16)],
        flops=3 * 2 * 1024 * 512 * W,
        name="query_gradient",
    )
    kv_plane = plane_gather(kv_own)
    dkv_keep, dkv_send = call(
        dkey_kernel,
        (shaped((2, ROWS, 2 * W), F32), shaped((2, ROWS, 2 * W), BF16)),
        place,
        stretch_ids,
        *kv_plane,
        qg_all,
        all_stats,
        smem=2,
        flops=4 * 2 * 1024 * 512 * W,
        name="key_value_gradient",
    )
    dq = plane_sum(dq_keep, dq_send).astype(BF16)
    dkv = plane_sum(dkv_keep, dkv_send).astype(BF16)

    moved = lax.ppermute(normed_rows, ("ctx", "tp"), TRANSPOSE)
    pair = jnp.concatenate([moved, lax.ppermute(moved, "tp", TP_X)], axis=0)
    up = lax.ppermute(pair, "tp", TP_UP)
    down = lax.ppermute(pair, "tp", TP_DOWN)
    up2 = lax.ppermute(up[:ROWS], "tp", TP_UP)
    down2 = lax.ppermute(down[ROWS:], "tp", TP_DOWN)
    turned = call(
        normed_kernel,
        shaped((640, PLANES * ROWS), BF16),
        place,
        pair,
        up,
        down,
        up2,
        down2,
        smem=1,
        name="normed_columns",
    )

    dkv_all = lax.all_gather(dkv, "ctx", axis=0, tiled=True, axis_index_groups=Z_GROUPS)
    dq_ring = ring(dq)
    q_keep, q_send = call(
        product_ring_kernel,
        (shaped((2, 160, W), F32), shaped((2, 160, W), BF16)),
        place,
        turned,
        *dq_ring,
        smem=1,
        scratch=[pltpu.VMEM((PLANES * ROWS, W), BF16)],
        flops=2 * 640 * 1024 * W,
        name="query_product",
    )
    kv_keep, kv_send = call(
        product,
        (shaped((2, 160, 2 * W), F32), shaped((2, 160, 2 * W), BF16)),
        place,
        turned,
        dkv_all,
        smem=1,
        flops=2 * 640 * 1024 * 2 * W,
        name="key_value_product",
    )
    q_out = row_sum(q_keep, q_send, xl).astype(BF16)
    kv_out = row_sum(kv_keep, kv_send, xl).astype(BF16)
    return (q_out, kv_out[:, :W], kv_out[:, W:])


def solution(mesh):
    return jax.shard_map(
        shards,
        mesh=mesh,
        in_specs=(
            P("ctx", "tp"),
            P("ctx", "tp"),
            P("ctx", "tp"),
            P("ctx", "tp"),
            P("ctx", "tp"),
            P(),
        ),
        out_specs=(P("ctx", "tp"), P("ctx", "tp"), P("ctx", "tp")),
        check_vma=False,
    )
```

```python
import functools
import math

import jax
import jax.numpy as jnp
from jax import lax
from jax.experimental import pallas as pl
from jax.experimental.pallas import tpu as pltpu
from jax.sharding import PartitionSpec as P

HD = 128
HEADS_DEV = 3
W = HD * HEADS_DEV
ROWS = 128
PLANES = 8
FACTOR = HD ** (-0.5)
SCALE2 = FACTOR * math.log2(math.e)
LOW = -1e30
F32 = jnp.float32
BF16 = jnp.bfloat16

CTX = 32
CORE_SWAP = [(i, i ^ 1) for i in range(CTX)]
X_SWAP = [(i, i ^ 2) for i in range(CTX)]
DIAG_SWAP = [(i, i ^ 3) for i in range(CTX)]
Z_UP = [(i, (i + 4) % CTX) for i in range(CTX)]
Z_DOWN = [(i, (i - 4) % CTX) for i in range(CTX)]
Z_GROUPS = [[4 * z + j for z in range(PLANES)] for j in range(4)]
TP_X = [(t, t ^ 4) for t in range(8)]
TP_UP = [(t, (t // 4) * 4 + (t + 1) % 4) for t in range(8)]
TP_DOWN = [(t, (t // 4) * 4 + (t + 3) % 4) for t in range(8)]
PLACES = [(z, j, t) for z in range(8) for j in range(4) for t in range(8)]
TURN_TP = [((4 * z + j) * 8 + t, (4 * z + j) * 8 + (t + z) % 8) for z, j, t in PLACES]
TURN_Z = [((4 * z + j) * 8 + t, (4 * ((t - z) % 8) + j) * 8 + t) for z, j, t in PLACES]

NT = (((1,), (1,)), ((), ()))
TN = (((0,), (0,)), ((), ()))
NN = (((1,), (0,)), ((), ()))


def dot(a, b, dims):
    return lax.dot_general(a, b, dims, preferred_element_type=F32)


RING_SHIFT = (0, -1, 1, -2, 2, -3, 3, 4)


def fill(scratch, refs):
    at = 0
    for ref in refs:
        n = ref.shape[0]
        scratch[at : at + n, :] = ref[...]
        at += n


def lane_row(values, width=ROWS):
    return jnp.concatenate([jnp.full((1, width), v, jnp.int32) for v in values], axis=1)


def fold(x, op):
    y = x.reshape(x.shape[0] // 8, 8, x.shape[1])
    return op(y, axis=0)


def plane_tables(place):
    z, xl = place[0], place[1]
    own = place[4 + 2 * z + xl]
    other = place[4 + 2 * z + 1 - xl]
    return [own, own, other, other]


def ring_tables(place):
    z, xl = place[0], place[1]
    return [place[4 + 2 * lax.rem(z + s + PLANES, PLANES) + xl] for s in RING_SHIFT]


def stats_kernel(place, *refs):
    qg, kv_in, out, sent = refs[:4], refs[4:13], refs[13], refs[14]
    qc, kc, sc = refs[15:]
    fill(qc, qg)
    fill(kc, kv_in)
    q_row = lane_row(plane_tables(place))
    k_st = ring_tables(place)
    out[...] = jnp.zeros_like(out)
    for h in range(HEADS_DEV):
        cols = slice(h * HD, (h + 1) * HD)
        gcols = slice(W + h * HD, W + (h + 1) * HD)
        qh = qc[:, cols]
        gh = qc[:, gcols]
        top = jnp.full((8, 4 * ROWS), LOW, F32)
        for k in range(PLANES):
            rows = slice(k * ROWS, (k + 1) * ROWS)
            s = dot(kc[rows, cols], qh, NT) * SCALE2
            s = jnp.where(q_row >= k_st[k], s, LOW)
            sc[rows, :] = s
            top = jnp.maximum(top, fold(s, jnp.max))
        m = jnp.maximum(jnp.max(top, axis=0, keepdims=True), 0.1 * LOW)
        total = jnp.zeros((8, 4 * ROWS), F32)
        weighted = jnp.zeros((8, 4 * ROWS), F32)
        for k in range(PLANES):
            rows = slice(k * ROWS, (k + 1) * ROWS)
            dp = dot(kc[rows, gcols], gh, NT)
            e = jnp.exp2(sc[rows, :] - m)
            total = total + fold(e, jnp.sum)
            weighted = weighted + fold(e * dp, jnp.sum)
        total = jnp.sum(total, axis=0, keepdims=True)
        weighted = jnp.sum(weighted, axis=0, keepdims=True)
        some = total > 0.0
        out[h : h + 1, :] = jnp.where(some, m + jnp.log2(total), 0.1 * LOW)
        out[3 + h : 4 + h, :] = jnp.where(some, weighted / total, 0.0)
    j = 2 * place[1] + place[2]
    for r in range(4):
        piece = out[:, r * ROWS : (r + 1) * ROWS]
        for i in range(PLANES):
            sent[4 * i + lax.bitwise_xor(j, r), :, :] = piece


def combine(parts):
    lse = [p[0:3] for p in parts]
    top = jnp.maximum(jnp.maximum(lse[0], lse[1]), jnp.maximum(lse[2], lse[3]))
    weights = [jnp.exp2(x - top) for x in lse]
    total = weights[0] + weights[1] + weights[2] + weights[3]
    delta = sum(w * p[3:6] for w, p in zip(weights, parts))
    return top + jnp.log2(total), delta / total


def dquery_kernel(place, *refs):
    qg, kv_in, stats = refs[:4], refs[4:13], refs[13:17]
    keep, send = refs[17:19]
    qc, kc, ds = refs[19:]
    fill(qc, qg)
    fill(kc, kv_in)
    q_row = lane_row(plane_tables(place))
    k_st = ring_tables(place)
    parts = []
    for d, ref in enumerate(stats):
        full = ref[...]
        parts.append(
            jnp.concatenate(
                [full[:, (r ^ d) * ROWS : ((r ^ d) + 1) * ROWS] for r in range(4)], axis=1
            )
        )
    all_lse, all_delta = combine(parts)
    for h in range(HEADS_DEV):
        cols = slice(h * HD, (h + 1) * HD)
        gcols = slice(W + h * HD, W + (h + 1) * HD)
        qh = qc[:, cols]
        gh = qc[:, gcols]
        lse = all_lse[h : h + 1, :]
        delta = all_delta[h : h + 1, :]
        for k in range(PLANES):
            rows = slice(k * ROWS, (k + 1) * ROWS)
            s = dot(kc[rows, cols], qh, NT) * SCALE2
            p = jnp.where(q_row >= k_st[k], jnp.exp2(s - lse), 0.0)
            dp = dot(kc[rows, gcols], gh, NT)
            ds[rows, :] = (FACTOR * p * (dp - delta)).astype(BF16)
        dq = dot(kc[:, cols], ds[...], TN).T
        for r in range(4):
            piece = dq[r * ROWS : (r + 1) * ROWS, :]
            if r % 2 == 0:
                keep[r // 2, :, cols] = piece
            else:
                send[r // 2, :, cols] = piece.astype(BF16)


def dkey_kernel(place, *refs):
    kv, qg, stats = refs[:4], refs[4], refs[5]
    keep, send = refs[6:]
    z, xl = place[0], place[1]
    q_row = lane_row([place[4 + 2 * i + xl] for i in range(PLANES)])
    k_st = plane_tables(place)
    all_lse, all_delta = combine(
        [jnp.concatenate([stats[4 * i + j] for i in range(PLANES)], axis=1) for j in range(4)]
    )
    for h in range(HEADS_DEV):
        cols = slice(h * HD, (h + 1) * HD)
        vcols = slice(W + h * HD, W + (h + 1) * HD)
        qh = qg[:, cols]
        gh = qg[:, vcols]
        lse = all_lse[h : h + 1, :]
        delta = all_delta[h : h + 1, :]
        for r in range(4):
            s = dot(kv[r][:, cols], qh, NT) * SCALE2
            p = jnp.where(q_row >= k_st[r], jnp.exp2(s - lse), 0.0)
            dp = dot(kv[r][:, vcols], gh, NT)
            ds = (FACTOR * p * (dp - delta)).astype(BF16)
            dv = dot(p.astype(BF16), gh, NN)
            dk = dot(ds, qh, NN)
            if r % 2 == 0:
                keep[r // 2, :, cols] = dk
                keep[r // 2, :, vcols] = dv
            else:
                send[r // 2, :, cols] = dk.astype(BF16)
                send[r // 2, :, vcols] = dv.astype(BF16)


def normed_kernel(place, pair, up, down, up2, down2, out):
    z, t = place[0], place[3]
    y = lax.rem(t, 4)
    xh = lax.div(t, 4)

    def put(block, hi, yy):
        plane = lax.rem(hi * 4 + lax.rem(yy + 4, 4) - z + PLANES, PLANES)
        out[:, pl.ds(pl.multiple_of(plane * ROWS, ROWS), ROWS)] = block.T

    for ref, dy in ((pair, 0), (up, -1), (down, 1)):
        put(ref[:ROWS, :], xh, y + dy)
        put(ref[ROWS:, :], 1 - xh, y + dy)
    put(up2[...], xh, y - 2)
    put(down2[...], 1 - xh, y + 2)


def product(place, at, b, keep, send):
    core = place[2]
    for half in range(2):
        mine = pl.multiple_of((2 * half + core) * 160, 160)
        theirs = pl.multiple_of((2 * half + 1 - core) * 160, 160)
        keep[half, :, :] = dot(at[pl.ds(mine, 160), :], b[...], NN)
        send[half, :, :] = dot(at[pl.ds(theirs, 160), :], b[...], NN).astype(BF16)


def call(kernel, out_shape, *args, scratch=(), smem=0, flops=0, name=None):
    specs = [pl.BlockSpec(memory_space=pltpu.SMEM)] * smem
    specs += [pl.BlockSpec(memory_space=pltpu.VMEM)] * (len(args) - smem)
    size = sum(math.prod(a.shape) * a.dtype.itemsize for a in args)
    return pl.pallas_call(
        kernel,
        out_shape=out_shape,
        in_specs=specs,
        out_specs=jax.tree.map(lambda _: pl.BlockSpec(memory_space=pltpu.VMEM), out_shape),
        scratch_shapes=list(scratch),
        compiler_params=pltpu.CompilerParams(vmem_limit_bytes=40 * 2**20),
        cost_estimate=pl.CostEstimate(flops=flops, bytes_accessed=size if flops else 0, transcendentals=0),
        name=name,
    )(*args)


def shaped(shape, dtype):
    return jax.ShapeDtypeStruct(shape, dtype)


def plane_gather(part):
    across = lax.ppermute(part, "ctx", X_SWAP)
    beside = lax.ppermute(part, "ctx", CORE_SWAP)
    diag = lax.ppermute(across, "ctx", CORE_SWAP)
    return [part, beside, across, diag]


def row_sum(keep, send, xl):
    got = lax.ppermute(send, "ctx", CORE_SWAP).astype(F32)
    both = keep + got
    mine = lax.dynamic_index_in_dim(both, xl, 0, keepdims=False)
    other = lax.dynamic_index_in_dim(both, 1 - xl, 0, keepdims=False).astype(BF16)
    return mine + lax.ppermute(other, "ctx", X_SWAP).astype(F32)


def after(value, *earlier):
    return lax.optimization_barrier((value, *earlier))[0]


def shards(normed_rows, query_rows, key_rows, value_rows, grad_output, stretch_ids):
    ctx = lax.axis_index("ctx")
    xl = lax.rem(lax.div(ctx, 2), 2)
    place = jnp.concatenate(
        [
            jnp.stack([lax.div(ctx, 4), xl, lax.rem(ctx, 2), lax.axis_index("tp")]).astype(
                jnp.int32
            ),
            stretch_ids,
        ]
    )
    half = ROWS // 2
    kv_own = jnp.concatenate([key_rows, value_rows], axis=1)
    qg_own = jnp.concatenate([query_rows, grad_output], axis=1)

    up1 = lax.ppermute(kv_own, "ctx", Z_UP)
    down1 = lax.ppermute(kv_own, "ctx", Z_DOWN)
    qg_plane = plane_gather(qg_own)
    turned_tp = lax.ppermute(normed_rows, ("ctx", "tp"), TURN_TP)
    up1, down1 = lax.optimization_barrier((up1, down1))
    up2 = lax.ppermute(up1, "ctx", Z_UP)
    down2 = lax.ppermute(down1, "ctx", Z_DOWN)
    up2, down2, qg_sent, turned_tp = lax.optimization_barrier((up2, down2, qg_own, turned_tp))
    qg_all = lax.all_gather(qg_sent, "ctx", axis=0, tiled=True, axis_index_groups=Z_GROUPS)
    up3 = lax.ppermute(up2, "ctx", Z_UP)
    down3 = lax.ppermute(down2, "ctx", Z_DOWN)
    up3, down3, kv_later, turned_tp = lax.optimization_barrier((up3, down3, kv_own, turned_tp))
    far_a = lax.ppermute(up3[:half], "ctx", Z_UP)
    far_b = lax.ppermute(down3[half:], "ctx", Z_DOWN)
    kv_plane = plane_gather(kv_later)
    kv_ring = [kv_own, up1, down1, up2, down2, up3, down3, far_a, far_b]

    wide = [
        pltpu.VMEM((4 * ROWS, 2 * W), BF16),
        pltpu.VMEM((PLANES * ROWS, 2 * W), BF16),
    ]
    stats, stats_sent = call(
        stats_kernel,
        (shaped((8, 4 * ROWS), F32), shaped((CTX, 8, ROWS), F32)),
        place,
        *qg_plane,
        *kv_ring,
        smem=1,
        scratch=wide + [pltpu.VMEM((PLANES * ROWS, 4 * ROWS), F32)],
        flops=2 * 2 * 1024 * 512 * W,
        name="softmax_statistics",
    )
    all_stats = lax.all_to_all(stats_sent, "ctx", split_axis=0, concat_axis=0, tiled=True)
    dq_keep, dq_send = call(
        dquery_kernel,
        (shaped((2, ROWS, W), F32), shaped((2, ROWS, W), BF16)),
        place,
        *qg_plane,
        *kv_ring,
        stats,
        lax.ppermute(stats, "ctx", CORE_SWAP),
        lax.ppermute(stats, "ctx", X_SWAP),
        lax.ppermute(stats, "ctx", DIAG_SWAP),
        smem=1,
        scratch=wide + [pltpu.VMEM((PLANES * ROWS, 4 * ROWS), BF16)],
        flops=0,
        name="query_gradient",
    )
    dq_got = lax.ppermute(dq_send, "ctx", CORE_SWAP).astype(F32)
    dq_other = (dq_keep[1] + dq_got[1]).astype(BF16)
    dkv_keep, dkv_send = call(
        dkey_kernel,
        (shaped((2, ROWS, 2 * W), F32), shaped((2, ROWS, 2 * W), BF16)),
        place,
        *kv_plane,
        qg_all,
        after(all_stats, dq_send),
        smem=1,
        flops=4 * 2 * 1024 * 512 * W,
        name="key_value_gradient",
    )
    dkv_got = lax.ppermute(dkv_send, "ctx", CORE_SWAP).astype(F32)
    dkv_other = (dkv_keep[1] + dkv_got[1]).astype(BF16)
    dkv = (
        dkv_keep[0] + dkv_got[0] + lax.ppermute(dkv_other, "ctx", X_SWAP).astype(F32)
    ).astype(BF16)
    dq = (
        dq_keep[0] + dq_got[0] + lax.ppermute(dq_other, "ctx", X_SWAP).astype(F32)
    ).astype(BF16)
    moved = lax.ppermute(after(turned_tp, dkv_send), ("ctx", "tp"), TURN_Z)
    grads = jnp.concatenate([dq, dkv], axis=1)
    grads_all = lax.all_gather(grads, "ctx", axis=0, tiled=True, axis_index_groups=Z_GROUPS)

    moved_x = lax.ppermute(moved, "tp", TP_X)
    pair = jnp.concatenate([moved, moved_x], axis=0)
    n_up = lax.ppermute(pair, "tp", TP_UP)
    n_down = lax.ppermute(pair, "tp", TP_DOWN)
    turned = call(
        normed_kernel,
        shaped((640, PLANES * ROWS), BF16),
        place,
        pair,
        n_up,
        n_down,
        lax.ppermute(n_up[:ROWS], "tp", TP_UP),
        lax.ppermute(n_down[ROWS:], "tp", TP_DOWN),
        smem=1,
        name="normed_columns",
    )
    keep, send = call(
        product,
        (shaped((2, 160, 3 * W), F32), shaped((2, 160, 3 * W), BF16)),
        place,
        turned,
        grads_all,
        smem=1,
        flops=2 * 640 * 1024 * 3 * W,
        name="weight_product",
    )
    out = row_sum(keep, send, xl).astype(BF16)
    return (out[:, :W], out[:, W : 2 * W], out[:, 2 * W :])


def solution(mesh):
    return jax.shard_map(
        shards,
        mesh=mesh,
        in_specs=(
            P("ctx", "tp"),
            P("ctx", "tp"),
            P("ctx", "tp"),
            P("ctx", "tp"),
            P("ctx", "tp"),
            P(),
        ),
        out_specs=(P("ctx", "tp"), P("ctx", "tp"), P("ctx", "tp")),
        check_vma=False,
    )
```

```python
import functools
import math

import jax
import jax.numpy as jnp
from jax import lax
from jax.experimental import pallas as pl
from jax.experimental.pallas import tpu as pltpu
from jax.sharding import PartitionSpec as P

HD = 128
HEADS_DEV = 3
W = HD * HEADS_DEV
ROWS = 128
PLANES = 8
FACTOR = HD ** (-0.5)
SCALE2 = FACTOR * math.log2(math.e)
LOW = -1e30
F32 = jnp.float32
BF16 = jnp.bfloat16

CTX = 32
CORE_SWAP = [(i, i ^ 1) for i in range(CTX)]
X_SWAP = [(i, i ^ 2) for i in range(CTX)]
DIAG_SWAP = [(i, i ^ 3) for i in range(CTX)]
Z_UP = [(i, (i + 4) % CTX) for i in range(CTX)]
Z_DOWN = [(i, (i - 4) % CTX) for i in range(CTX)]
Z_GROUPS = [[4 * z + j for z in range(PLANES)] for j in range(4)]
TP_X = [(t, t ^ 4) for t in range(8)]
TP_UP = [(t, (t // 4) * 4 + (t + 1) % 4) for t in range(8)]
TP_DOWN = [(t, (t // 4) * 4 + (t + 3) % 4) for t in range(8)]
PLACES = [(z, j, t) for z in range(8) for j in range(4) for t in range(8)]
TURN_TP = [((4 * z + j) * 8 + t, (4 * z + j) * 8 + (t + z) % 8) for z, j, t in PLACES]
TURN_Z = [((4 * z + j) * 8 + t, (4 * ((t - z) % 8) + j) * 8 + t) for z, j, t in PLACES]

NT = (((1,), (1,)), ((), ()))
TN = (((0,), (0,)), ((), ()))
NN = (((1,), (0,)), ((), ()))


def dot(a, b, dims):
    return lax.dot_general(a, b, dims, preferred_element_type=F32)


RING_SHIFT = (0, -1, 1, -2, 2, -3, 3, 4)


def fill(scratch, refs):
    at = 0
    for ref in refs:
        n = ref.shape[0]
        scratch[at : at + n, :] = ref[...]
        at += n


def lane_row(values, width=ROWS):
    return jnp.concatenate([jnp.full((1, width), v, jnp.int32) for v in values], axis=1)


def fold(x, op):
    y = x.reshape(x.shape[0] // 8, 8, x.shape[1])
    return op(y, axis=0)


def plane_tables(place):
    z, xl = place[0], place[1]
    own = place[4 + 2 * z + xl]
    other = place[4 + 2 * z + 1 - xl]
    return [own, own, other, other]


def ring_tables(place):
    z, xl = place[0], place[1]
    return [place[4 + 2 * lax.rem(z + s + PLANES, PLANES) + xl] for s in RING_SHIFT]


def subset_stats(qc, kc, sc, q_row, k_st, out):
    out[...] = jnp.zeros_like(out)
    for h in range(HEADS_DEV):
        cols = slice(h * HD, (h + 1) * HD)
        gcols = slice(W + h * HD, W + (h + 1) * HD)
        qh = qc[:, cols]
        gh = qc[:, gcols]
        top = jnp.full((8, 4 * ROWS), LOW, F32)
        for k, stretch in enumerate(k_st):
            rows = slice(k * ROWS, (k + 1) * ROWS)
            s = dot(kc[rows, cols], qh, NT) * SCALE2
            s = jnp.where(q_row >= stretch, s, LOW)
            sc[rows, :] = s
            top = jnp.maximum(top, fold(s, jnp.max))
        m = jnp.maximum(jnp.max(top, axis=0, keepdims=True), 0.1 * LOW)
        total = jnp.zeros((8, 4 * ROWS), F32)
        weighted = jnp.zeros((8, 4 * ROWS), F32)
        for k in range(len(k_st)):
            rows = slice(k * ROWS, (k + 1) * ROWS)
            dp = dot(kc[rows, gcols], gh, NT)
            e = jnp.exp2(sc[rows, :] - m)
            total = total + fold(e, jnp.sum)
            weighted = weighted + fold(e * dp, jnp.sum)
        total = jnp.sum(total, axis=0, keepdims=True)
        weighted = jnp.sum(weighted, axis=0, keepdims=True)
        some = total > 0.0
        out[h : h + 1, :] = jnp.where(some, m + jnp.log2(total), 0.1 * LOW)
        out[3 + h : 4 + h, :] = jnp.where(some, weighted / total, 0.0)


def near_stats_kernel(place, *refs):
    qg, kv_in, out = refs[:4], refs[4:11], refs[11]
    qc, kc, sc = refs[12:]
    fill(qc, qg)
    fill(kc, kv_in)
    subset_stats(qc, kc, sc, lane_row(plane_tables(place)), ring_tables(place)[:7], out)


def stats_kernel(place, *refs):
    qg, kv_in, near, out, sent = refs[:4], refs[4:6], refs[6], refs[7], refs[8]
    qc, kc, sc = refs[9:]
    fill(qc, qg)
    fill(kc, kv_in)
    subset_stats(qc, kc, sc, lane_row(plane_tables(place)), ring_tables(place)[7:], out)
    lse, delta = combine([near[...], out[...]])
    out[0:3, :] = lse
    out[3:6, :] = delta
    j = 2 * place[1] + place[2]
    for r in range(4):
        piece = out[:, r * ROWS : (r + 1) * ROWS]
        for i in range(PLANES):
            sent[4 * i + lax.bitwise_xor(j, r), :, :] = piece


def combine(parts):
    top = functools.reduce(jnp.maximum, [p[0:3] for p in parts])
    weights = [jnp.exp2(p[0:3] - top) for p in parts]
    total = sum(weights)
    delta = sum(w * p[3:6] for w, p in zip(weights, parts))
    return top + jnp.log2(total), delta / total


def dquery_kernel(place, *refs):
    qg, kv_in, stats = refs[:4], refs[4:13], refs[13:17]
    keep, send = refs[17:19]
    qc, kc, ds = refs[19:]
    fill(qc, qg)
    fill(kc, kv_in)
    q_row = lane_row(plane_tables(place))
    k_st = ring_tables(place)
    parts = []
    for d, ref in enumerate(stats):
        full = ref[...]
        parts.append(
            jnp.concatenate(
                [full[:, (r ^ d) * ROWS : ((r ^ d) + 1) * ROWS] for r in range(4)], axis=1
            )
        )
    all_lse, all_delta = combine(parts)
    for h in range(HEADS_DEV):
        cols = slice(h * HD, (h + 1) * HD)
        gcols = slice(W + h * HD, W + (h + 1) * HD)
        qh = qc[:, cols]
        gh = qc[:, gcols]
        lse = all_lse[h : h + 1, :]
        delta = all_delta[h : h + 1, :]
        for k in range(PLANES):
            rows = slice(k * ROWS, (k + 1) * ROWS)
            s = dot(kc[rows, cols], qh, NT) * SCALE2
            p = jnp.where(q_row >= k_st[k], jnp.exp2(s - lse), 0.0)
            dp = dot(kc[rows, gcols], gh, NT)
            ds[rows, :] = (FACTOR * p * (dp - delta)).astype(BF16)
        dq = dot(kc[:, cols], ds[...], TN).T
        for r in range(4):
            piece = dq[r * ROWS : (r + 1) * ROWS, :]
            if r % 2 == 0:
                keep[r // 2, :, cols] = piece
            else:
                send[r // 2, :, cols] = piece.astype(BF16)


def dkey_kernel(pieces, place, *refs):
    count = len(pieces)
    kv, qg, stats, outs = refs[:count], refs[count], refs[count + 1], refs[count + 2]
    z, xl = place[0], place[1]
    q_row = lane_row([place[4 + 2 * i + xl] for i in range(PLANES)])
    k_st = plane_tables(place)
    all_lse, all_delta = combine(
        [jnp.concatenate([stats[4 * i + j] for i in range(PLANES)], axis=1) for j in range(4)]
    )
    for h in range(HEADS_DEV):
        cols = slice(h * HD, (h + 1) * HD)
        vcols = slice(W + h * HD, W + (h + 1) * HD)
        qh = qg[:, cols]
        gh = qg[:, vcols]
        lse = all_lse[h : h + 1, :]
        delta = all_delta[h : h + 1, :]
        for n, r in enumerate(pieces):
            s = dot(kv[n][:, cols], qh, NT) * SCALE2
            p = jnp.where(q_row >= k_st[r], jnp.exp2(s - lse), 0.0)
            dp = dot(kv[n][:, vcols], gh, NT)
            ds = (FACTOR * p * (dp - delta)).astype(BF16)
            outs[n, :, cols] = dot(ds, qh, NN).astype(outs.dtype)
            outs[n, :, vcols] = dot(p.astype(BF16), gh, NN).astype(outs.dtype)


def normed_kernel(place, pair, up, down, up2, down2, out):
    z, t = place[0], place[3]
    y = lax.rem(t, 4)
    xh = lax.div(t, 4)

    def put(block, hi, yy):
        plane = lax.rem(hi * 4 + lax.rem(yy + 4, 4) - z + PLANES, PLANES)
        out[:, pl.ds(pl.multiple_of(plane * ROWS, ROWS), ROWS)] = block.T

    for ref, dy in ((pair, 0), (up, -1), (down, 1)):
        put(ref[:ROWS, :], xh, y + dy)
        put(ref[ROWS:, :], 1 - xh, y + dy)
    put(up2[...], xh, y - 2)
    put(down2[...], 1 - xh, y + 2)


def product_kernel(place, at, rows, *outs):
    core = place[2]
    for part in range(3):
        keep, send = outs[2 * part], outs[2 * part + 1]
        cols = slice(part * W, (part + 1) * W)
        for half in range(2):
            theirs = pl.multiple_of((2 * half + 1 - core) * 160, 160)
            mine = pl.multiple_of((2 * half + core) * 160, 160)
            send[half, :, :] = dot(at[pl.ds(theirs, 160), :], rows[:, cols], NN).astype(BF16)
            keep[half, :, :] = dot(at[pl.ds(mine, 160), :], rows[:, cols], NN)


def call(kernel, out_shape, *args, scratch=(), smem=0, flops=0, name=None):
    specs = [pl.BlockSpec(memory_space=pltpu.SMEM)] * smem
    specs += [pl.BlockSpec(memory_space=pltpu.VMEM)] * (len(args) - smem)
    size = sum(math.prod(a.shape) * a.dtype.itemsize for a in args)
    return pl.pallas_call(
        kernel,
        out_shape=out_shape,
        in_specs=specs,
        out_specs=jax.tree.map(lambda _: pl.BlockSpec(memory_space=pltpu.VMEM), out_shape),
        scratch_shapes=list(scratch),
        compiler_params=pltpu.CompilerParams(vmem_limit_bytes=20 * 2**20),
        cost_estimate=pl.CostEstimate(flops=flops, bytes_accessed=size if flops else 0, transcendentals=0),
        name=name,
    )(*args)


def shaped(shape, dtype):
    return jax.ShapeDtypeStruct(shape, dtype)


def plane_gather(part):
    across = lax.ppermute(part, "ctx", X_SWAP)
    beside = lax.ppermute(part, "ctx", CORE_SWAP)
    diag = lax.ppermute(across, "ctx", CORE_SWAP)
    return [part, beside, across, diag]


def row_sum(keep, send, xl):
    got = lax.ppermute(send, "ctx", CORE_SWAP).astype(F32)
    both = keep + got
    mine = lax.dynamic_index_in_dim(both, xl, 0, keepdims=False)
    other = lax.dynamic_index_in_dim(both, 1 - xl, 0, keepdims=False).astype(BF16)
    return mine + lax.ppermute(other, "ctx", X_SWAP).astype(F32)


def after(value, *earlier):
    return lax.optimization_barrier((value, *earlier))[0]


def shards(normed_rows, query_rows, key_rows, value_rows, grad_output, stretch_ids):
    ctx = lax.axis_index("ctx")
    xl = lax.rem(lax.div(ctx, 2), 2)
    place = jnp.concatenate(
        [
            jnp.stack([lax.div(ctx, 4), xl, lax.rem(ctx, 2), lax.axis_index("tp")]).astype(
                jnp.int32
            ),
            stretch_ids,
        ]
    )
    half = ROWS // 2
    kv_own = jnp.concatenate([key_rows, value_rows], axis=1)
    qg_own = jnp.concatenate([query_rows, grad_output], axis=1)

    up1 = lax.ppermute(kv_own, "ctx", Z_UP)
    down1 = lax.ppermute(kv_own, "ctx", Z_DOWN)
    qg_plane = plane_gather(qg_own)
    turned_tp = lax.ppermute(normed_rows, ("ctx", "tp"), TURN_TP)
    up1, down1 = lax.optimization_barrier((up1, down1))
    up2 = lax.ppermute(up1, "ctx", Z_UP)
    down2 = lax.ppermute(down1, "ctx", Z_DOWN)
    up2, down2, qg_sent, turned_tp = lax.optimization_barrier((up2, down2, qg_own, turned_tp))
    qg_all = lax.all_gather(qg_sent, "ctx", axis=0, tiled=True, axis_index_groups=Z_GROUPS)
    up3 = lax.ppermute(up2, "ctx", Z_UP)
    down3 = lax.ppermute(down2, "ctx", Z_DOWN)
    up3, down3, kv_later, turned_tp = lax.optimization_barrier((up3, down3, kv_own, turned_tp))
    far_a = lax.ppermute(up3[:half], "ctx", Z_UP)
    far_b = lax.ppermute(down3[half:], "ctx", Z_DOWN)
    kv_plane = plane_gather(kv_later)
    qg_plane[0] = jnp.concatenate([after(query_rows, up2), grad_output], axis=1)
    kv_ring = [kv_own, up1, down1, up2, down2, up3, down3, far_a, far_b]

    wide = [
        pltpu.VMEM((4 * ROWS, 2 * W), BF16),
        pltpu.VMEM((PLANES * ROWS, 2 * W), BF16),
    ]
    near_stats = call(
        near_stats_kernel,
        shaped((8, 4 * ROWS), F32),
        place,
        *qg_plane,
        *kv_ring[:7],
        smem=1,
        scratch=[
            wide[0],
            pltpu.VMEM((7 * ROWS, 2 * W), BF16),
            pltpu.VMEM((7 * ROWS, 4 * ROWS), F32),
        ],
        flops=2 * 2 * 896 * 512 * W,
        name="near_statistics",
    )
    stats, stats_sent = call(
        stats_kernel,
        (shaped((8, 4 * ROWS), F32), shaped((CTX, 8, ROWS), F32)),
        place,
        *qg_plane,
        *kv_ring[7:],
        near_stats,
        smem=1,
        scratch=[
            wide[0],
            pltpu.VMEM((ROWS, 2 * W), BF16),
            pltpu.VMEM((ROWS, 4 * ROWS), F32),
        ],
        flops=2 * 2 * 128 * 512 * W,
        name="softmax_statistics",
    )
    all_stats = lax.all_to_all(stats_sent, "ctx", split_axis=0, concat_axis=0, tiled=True)
    dq_keep, dq_send = call(
        dquery_kernel,
        (shaped((2, ROWS, W), F32), shaped((2, ROWS, W), BF16)),
        place,
        *qg_plane,
        *kv_ring,
        stats,
        lax.ppermute(stats, "ctx", CORE_SWAP),
        lax.ppermute(stats, "ctx", X_SWAP),
        lax.ppermute(stats, "ctx", DIAG_SWAP),
        smem=1,
        scratch=wide + [pltpu.VMEM((PLANES * ROWS, 4 * ROWS), BF16)],
        flops=0,
        name="query_gradient",
    )
    dq_got = lax.ppermute(dq_send, "ctx", CORE_SWAP).astype(F32)
    def key_value_gradient(pieces, dtype, name):
        return call(
            functools.partial(dkey_kernel, pieces),
            shaped((len(pieces), ROWS, 2 * W), dtype),
            place,
            *[kv_plane[r] for r in pieces],
            qg_all,
            all_stats,
            smem=1,
            flops=len(pieces) * 2 * 1024 * 512 * W,
            name=name,
        )

    all_stats = after(all_stats, dq_send)
    dkv_send = key_value_gradient((1, 3), BF16, "core_gradient")
    all_stats = after(all_stats, dkv_send)
    dkv_across = key_value_gradient((2,), F32, "across_gradient")
    all_stats = after(all_stats, dkv_across)
    dkv_own = key_value_gradient((0,), F32, "own_gradient")
    dq_other = (dq_keep[1] + dq_got[1]).astype(BF16)
    dq_x = lax.ppermute(dq_other, "ctx", X_SWAP).astype(F32)
    dkv_got = lax.ppermute(dkv_send, "ctx", CORE_SWAP).astype(F32)
    dkv_other = (dkv_across[0] + dkv_got[1]).astype(BF16)
    dkv_x = lax.ppermute(dkv_other, "ctx", X_SWAP).astype(F32)
    dq = dq_keep[0] + dq_got[0] + dq_x
    dkv = dkv_own[0] + dkv_got[0] + dkv_x
    grads = jnp.concatenate([dq, dkv], axis=1).astype(BF16)
    moved = lax.ppermute(after(turned_tp, dkv_send), ("ctx", "tp"), TURN_Z)
    grads_all = lax.all_gather(grads, "ctx", axis=0, tiled=True, axis_index_groups=Z_GROUPS)

    moved_x = lax.ppermute(moved, "tp", TP_X)
    pair = jnp.concatenate([moved, moved_x], axis=0)
    n_up = lax.ppermute(pair, "tp", TP_UP)
    n_down = lax.ppermute(pair, "tp", TP_DOWN)
    turned = call(
        normed_kernel,
        shaped((640, PLANES * ROWS), BF16),
        place,
        pair,
        n_up,
        n_down,
        lax.ppermute(n_up[:ROWS], "tp", TP_UP),
        lax.ppermute(n_down[ROWS:], "tp", TP_DOWN),
        smem=1,
        name="normed_columns",
    )
    sums = call(
        product_kernel,
        (shaped((2, 160, W), F32), shaped((2, 160, W), BF16)) * 3,
        place,
        turned,
        grads_all,
        smem=1,
        flops=2 * 640 * 1024 * 3 * W,
        name="weight_product",
    )
    return tuple(row_sum(sums[2 * i], sums[2 * i + 1], xl).astype(BF16) for i in range(3))


def solution(mesh):
    return jax.shard_map(
        shards,
        mesh=mesh,
        in_specs=(
            P("ctx", "tp"),
            P("ctx", "tp"),
            P("ctx", "tp"),
            P("ctx", "tp"),
            P("ctx", "tp"),
            P(),
        ),
        out_specs=(P("ctx", "tp"), P("ctx", "tp"), P("ctx", "tp")),
        check_vma=False,
    )
```

```python
import functools
import math

import jax
import jax.numpy as jnp
from jax import lax
from jax.experimental import pallas as pl
from jax.experimental.pallas import tpu as pltpu
from jax.sharding import PartitionSpec as P

HD = 128
HEADS_DEV = 3
W = HD * HEADS_DEV
ROWS = 128
PLANES = 8
FACTOR = HD ** (-0.5)
SCALE2 = FACTOR * math.log2(math.e)
LOW = -1e30
F32 = jnp.float32
BF16 = jnp.bfloat16

CTX = 32
CORE_SWAP = [(i, i ^ 1) for i in range(CTX)]
X_SWAP = [(i, i ^ 2) for i in range(CTX)]
DIAG_SWAP = [(i, i ^ 3) for i in range(CTX)]
Z_UP = [(i, (i + 4) % CTX) for i in range(CTX)]
Z_DOWN = [(i, (i - 4) % CTX) for i in range(CTX)]
Z_GROUPS = [[4 * z + j for z in range(PLANES)] for j in range(4)]
TP_X = [(t, t ^ 4) for t in range(8)]
TP_UP = [(t, (t // 4) * 4 + (t + 1) % 4) for t in range(8)]
TP_DOWN = [(t, (t // 4) * 4 + (t + 3) % 4) for t in range(8)]
PLACES = [(z, j, t) for z in range(8) for j in range(4) for t in range(8)]
TURN_TP = [((4 * z + j) * 8 + t, (4 * z + j) * 8 + (t + z) % 8) for z, j, t in PLACES]
TURN_Z = [((4 * z + j) * 8 + t, (4 * ((t - z) % 8) + j) * 8 + t) for z, j, t in PLACES]

NT = (((1,), (1,)), ((), ()))
TN = (((0,), (0,)), ((), ()))
NN = (((1,), (0,)), ((), ()))


def dot(a, b, dims):
    return lax.dot_general(a, b, dims, preferred_element_type=F32)


RING_SHIFT = (0, -1, 1, -2, 2, -3, 3, 4)


def fill(scratch, refs):
    at = 0
    for ref in refs:
        n = ref.shape[0]
        scratch[at : at + n, :] = ref[...]
        at += n


def lane_row(values, width=ROWS):
    return jnp.concatenate([jnp.full((1, width), v, jnp.int32) for v in values], axis=1)


def fold(x, op):
    y = x.reshape(x.shape[0] // 8, 8, x.shape[1])
    return op(y, axis=0)


def plane_tables(place):
    z, xl = place[0], place[1]
    own = place[4 + 2 * z + xl]
    other = place[4 + 2 * z + 1 - xl]
    return [own, own, other, other]


def ring_tables(place):
    z, xl = place[0], place[1]
    return [place[4 + 2 * lax.rem(z + s + PLANES, PLANES) + xl] for s in RING_SHIFT]


def subset_stats(qc, kc, sc, q_row, k_st, out):
    out[...] = jnp.zeros_like(out)
    for h in range(HEADS_DEV):
        cols = slice(h * HD, (h + 1) * HD)
        gcols = slice(W + h * HD, W + (h + 1) * HD)
        qh = qc[:, cols]
        gh = qc[:, gcols]
        top = jnp.full((8, 4 * ROWS), LOW, F32)
        for k, stretch in enumerate(k_st):
            rows = slice(k * ROWS, (k + 1) * ROWS)
            s = dot(kc[rows, cols], qh, NT) * SCALE2
            s = jnp.where(q_row >= stretch, s, LOW)
            sc[rows, :] = s
            top = jnp.maximum(top, fold(s, jnp.max))
        m = jnp.maximum(jnp.max(top, axis=0, keepdims=True), 0.1 * LOW)
        total = jnp.zeros((8, 4 * ROWS), F32)
        weighted = jnp.zeros((8, 4 * ROWS), F32)
        for k in range(len(k_st)):
            rows = slice(k * ROWS, (k + 1) * ROWS)
            dp = dot(kc[rows, gcols], gh, NT)
            e = jnp.exp2(sc[rows, :] - m)
            total = total + fold(e, jnp.sum)
            weighted = weighted + fold(e * dp, jnp.sum)
        total = jnp.sum(total, axis=0, keepdims=True)
        weighted = jnp.sum(weighted, axis=0, keepdims=True)
        some = total > 0.0
        out[h : h + 1, :] = jnp.where(some, m + jnp.log2(total), 0.1 * LOW)
        out[3 + h : 4 + h, :] = jnp.where(some, weighted / total, 0.0)


def near_stats_kernel(place, *refs):
    qg, kv_in, out = refs[:4], refs[4:11], refs[11]
    qc, kc, sc = refs[12:]
    fill(qc, qg)
    fill(kc, kv_in)
    subset_stats(qc, kc, sc, lane_row(plane_tables(place)), ring_tables(place)[:7], out)


def stats_kernel(place, *refs):
    qg, kv_in, near, out, sent = refs[:4], refs[4:6], refs[6], refs[7], refs[8]
    qc, kc, sc = refs[9:]
    fill(qc, qg)
    fill(kc, kv_in)
    subset_stats(qc, kc, sc, lane_row(plane_tables(place)), ring_tables(place)[7:], out)
    lse, delta = combine([near[...], out[...]])
    out[0:3, :] = lse
    out[3:6, :] = delta
    j = 2 * place[1] + place[2]
    for r in range(4):
        piece = out[:, r * ROWS : (r + 1) * ROWS]
        for i in range(PLANES):
            sent[4 * i + lax.bitwise_xor(j, r), :, :] = piece


def combine(parts):
    top = functools.reduce(jnp.maximum, [p[0:3] for p in parts])
    weights = [jnp.exp2(p[0:3] - top) for p in parts]
    total = sum(weights)
    delta = sum(w * p[3:6] for w, p in zip(weights, parts))
    return top + jnp.log2(total), delta / total


def dquery_kernel(place, *refs):
    qg, kv_in, stats = refs[:4], refs[4:13], refs[13:17]
    keep, send = refs[17:19]
    qc, kc, ds = refs[19:]
    fill(qc, qg)
    fill(kc, kv_in)
    q_row = lane_row(plane_tables(place))
    k_st = ring_tables(place)
    parts = []
    for d, ref in enumerate(stats):
        full = ref[...]
        parts.append(
            jnp.concatenate(
                [full[:, (r ^ d) * ROWS : ((r ^ d) + 1) * ROWS] for r in range(4)], axis=1
            )
        )
    all_lse, all_delta = combine(parts)
    for h in range(HEADS_DEV):
        cols = slice(h * HD, (h + 1) * HD)
        gcols = slice(W + h * HD, W + (h + 1) * HD)
        qh = qc[:, cols]
        gh = qc[:, gcols]
        lse = all_lse[h : h + 1, :]
        delta = all_delta[h : h + 1, :]
        for k in range(PLANES):
            rows = slice(k * ROWS, (k + 1) * ROWS)
            s = dot(kc[rows, cols], qh, NT) * SCALE2
            p = jnp.where(q_row >= k_st[k], jnp.exp2(s - lse), 0.0)
            dp = dot(kc[rows, gcols], gh, NT)
            ds[rows, :] = (FACTOR * p * (dp - delta)).astype(BF16)
        dq = dot(kc[:, cols], ds[...], TN).T
        for r in range(4):
            piece = dq[r * ROWS : (r + 1) * ROWS, :]
            if r % 2 == 0:
                keep[r // 2, :, cols] = piece
            else:
                send[r // 2, :, cols] = piece.astype(BF16)


def dkey_kernel(pieces, place, *refs):
    count = len(pieces)
    kv, qg, stats, outs = refs[:count], refs[count], refs[count + 1], refs[count + 2]
    z, xl = place[0], place[1]
    q_row = lane_row([place[4 + 2 * i + xl] for i in range(PLANES)])
    k_st = plane_tables(place)
    all_lse, all_delta = combine(
        [jnp.concatenate([stats[4 * i + j] for i in range(PLANES)], axis=1) for j in range(4)]
    )
    for h in range(HEADS_DEV):
        cols = slice(h * HD, (h + 1) * HD)
        vcols = slice(W + h * HD, W + (h + 1) * HD)
        qh = qg[:, cols]
        gh = qg[:, vcols]
        lse = all_lse[h : h + 1, :]
        delta = all_delta[h : h + 1, :]
        for n, r in enumerate(pieces):
            s = dot(kv[n][:, cols], qh, NT) * SCALE2
            p = jnp.where(q_row >= k_st[r], jnp.exp2(s - lse), 0.0)
            dp = dot(kv[n][:, vcols], gh, NT)
            ds = (FACTOR * p * (dp - delta)).astype(BF16)
            outs[n, :, cols] = dot(ds, qh, NN).astype(outs.dtype)
            outs[n, :, vcols] = dot(p.astype(BF16), gh, NN).astype(outs.dtype)


def normed_kernel(place, pair, up, down, up2, down2, out):
    z, t = place[0], place[3]
    y = lax.rem(t, 4)
    xh = lax.div(t, 4)

    def put(block, hi, yy):
        plane = lax.rem(hi * 4 + lax.rem(yy + 4, 4) - z + PLANES, PLANES)
        out[:, pl.ds(pl.multiple_of(plane * ROWS, ROWS), ROWS)] = block.T

    for ref, dy in ((pair, 0), (up, -1), (down, 1)):
        put(ref[:ROWS, :], xh, y + dy)
        put(ref[ROWS:, :], 1 - xh, y + dy)
    put(up2[...], xh, y - 2)
    put(down2[...], 1 - xh, y + 2)


def product_kernel(place, at, rows, *outs):
    core = place[2]
    for part in range(3):
        keep, send = outs[2 * part], outs[2 * part + 1]
        cols = slice(part * W, (part + 1) * W)
        for half in range(2):
            theirs = pl.multiple_of((2 * half + 1 - core) * 160, 160)
            mine = pl.multiple_of((2 * half + core) * 160, 160)
            send[half, :, :] = dot(at[pl.ds(theirs, 160), :], rows[:, cols], NN).astype(BF16)
            keep[half, :, :] = dot(at[pl.ds(mine, 160), :], rows[:, cols], NN)


def call(kernel, out_shape, *args, scratch=(), smem=0, flops=0, name=None):
    specs = [pl.BlockSpec(memory_space=pltpu.SMEM)] * smem
    specs += [pl.BlockSpec(memory_space=pltpu.VMEM)] * (len(args) - smem)
    size = sum(math.prod(a.shape) * a.dtype.itemsize for a in args)
    return pl.pallas_call(
        kernel,
        out_shape=out_shape,
        in_specs=specs,
        out_specs=jax.tree.map(lambda _: pl.BlockSpec(memory_space=pltpu.VMEM), out_shape),
        scratch_shapes=list(scratch),
        compiler_params=pltpu.CompilerParams(vmem_limit_bytes=20 * 2**20),
        cost_estimate=pl.CostEstimate(flops=flops, bytes_accessed=size if flops else 0, transcendentals=0),
        name=name,
    )(*args)


def shaped(shape, dtype):
    return jax.ShapeDtypeStruct(shape, dtype)


def plane_gather(part):
    across = lax.ppermute(part, "ctx", X_SWAP)
    beside = lax.ppermute(part, "ctx", CORE_SWAP)
    diag = lax.ppermute(across, "ctx", CORE_SWAP)
    return [part, beside, across, diag]


def row_sum(keep, send, xl):
    got = lax.ppermute(send, "ctx", CORE_SWAP).astype(F32)
    both = keep + got
    mine = lax.dynamic_index_in_dim(both, xl, 0, keepdims=False)
    other = lax.dynamic_index_in_dim(both, 1 - xl, 0, keepdims=False).astype(BF16)
    return mine + lax.ppermute(other, "ctx", X_SWAP).astype(F32)


def after(value, *earlier):
    return lax.optimization_barrier((value, *earlier))[0]


def shards(normed_rows, query_rows, key_rows, value_rows, grad_output, stretch_ids):
    ctx = lax.axis_index("ctx")
    xl = lax.rem(lax.div(ctx, 2), 2)
    place = jnp.concatenate(
        [
            jnp.stack([lax.div(ctx, 4), xl, lax.rem(ctx, 2), lax.axis_index("tp")]).astype(
                jnp.int32
            ),
            stretch_ids,
        ]
    )
    half = ROWS // 2
    kv_own = jnp.concatenate([key_rows, value_rows], axis=1)
    qg_own = jnp.concatenate([query_rows, grad_output], axis=1)

    up1 = lax.ppermute(kv_own, "ctx", Z_UP)
    down1 = lax.ppermute(kv_own, "ctx", Z_DOWN)
    qg_plane = plane_gather(qg_own)
    turned_tp = lax.ppermute(normed_rows, ("ctx", "tp"), TURN_TP)
    up1, down1, qg_sent, turned_tp = lax.optimization_barrier(
        (up1, down1, qg_own, turned_tp)
    )
    qg_all = lax.all_gather(qg_sent, "ctx", axis=0, tiled=True, axis_index_groups=Z_GROUPS)
    up2 = lax.ppermute(up1, "ctx", Z_UP)
    down2 = lax.ppermute(down1, "ctx", Z_DOWN)
    up2, down2 = lax.optimization_barrier((up2, down2))
    up3 = lax.ppermute(up2, "ctx", Z_UP)
    down3 = lax.ppermute(down2, "ctx", Z_DOWN)
    up3, down3, kv_later = lax.optimization_barrier((up3, down3, kv_own))
    far_a = lax.ppermute(up3[:half], "ctx", Z_UP)
    far_b = lax.ppermute(down3[half:], "ctx", Z_DOWN)
    kv_plane = plane_gather(kv_later)
    qg_plane[0] = jnp.concatenate([after(query_rows, up2), grad_output], axis=1)
    kv_ring = [kv_own, up1, down1, up2, down2, up3, down3, far_a, far_b]

    wide = [
        pltpu.VMEM((4 * ROWS, 2 * W), BF16),
        pltpu.VMEM((PLANES * ROWS, 2 * W), BF16),
    ]
    near_stats = call(
        near_stats_kernel,
        shaped((8, 4 * ROWS), F32),
        place,
        *qg_plane,
        *kv_ring[:7],
        smem=1,
        scratch=[
            wide[0],
            pltpu.VMEM((7 * ROWS, 2 * W), BF16),
            pltpu.VMEM((7 * ROWS, 4 * ROWS), F32),
        ],
        flops=2 * 2 * 896 * 512 * W,
        name="near_statistics",
    )
    stats, stats_sent = call(
        stats_kernel,
        (shaped((8, 4 * ROWS), F32), shaped((CTX, 8, ROWS), F32)),
        place,
        *qg_plane,
        *kv_ring[7:],
        near_stats,
        smem=1,
        scratch=[
            wide[0],
            pltpu.VMEM((ROWS, 2 * W), BF16),
            pltpu.VMEM((ROWS, 4 * ROWS), F32),
        ],
        flops=2 * 2 * 128 * 512 * W,
        name="softmax_statistics",
    )
    all_stats = lax.all_to_all(stats_sent, "ctx", split_axis=0, concat_axis=0, tiled=True)
    dq_keep, dq_send = call(
        dquery_kernel,
        (shaped((2, ROWS, W), F32), shaped((2, ROWS, W), BF16)),
        place,
        *qg_plane,
        *kv_ring,
        stats,
        lax.ppermute(stats, "ctx", CORE_SWAP),
        lax.ppermute(stats, "ctx", X_SWAP),
        lax.ppermute(stats, "ctx", DIAG_SWAP),
        smem=1,
        scratch=wide + [pltpu.VMEM((PLANES * ROWS, 4 * ROWS), BF16)],
        flops=0,
        name="query_gradient",
    )
    dq_got = lax.ppermute(dq_send, "ctx", CORE_SWAP).astype(F32)
    def key_value_gradient(pieces, dtype, name):
        return call(
            functools.partial(dkey_kernel, pieces),
            shaped((len(pieces), ROWS, 2 * W), dtype),
            place,
            *[kv_plane[r] for r in pieces],
            qg_all,
            all_stats,
            smem=1,
            flops=len(pieces) * 2 * 1024 * 512 * W,
            name=name,
        )

    all_stats = after(all_stats, dq_send)
    dkv_send = key_value_gradient((1, 3), BF16, "core_gradient")
    all_stats = after(all_stats, dkv_send)
    dkv_across = key_value_gradient((2,), F32, "across_gradient")
    all_stats = after(all_stats, dkv_across)
    dkv_own = key_value_gradient((0,), F32, "own_gradient")
    dq_other = (dq_keep[1] + dq_got[1]).astype(BF16)
    dq_x = lax.ppermute(dq_other, "ctx", X_SWAP).astype(F32)
    dkv_got = lax.ppermute(dkv_send, "ctx", CORE_SWAP).astype(F32)
    dkv_other = (dkv_across[0] + dkv_got[1]).astype(BF16)
    dkv_x = lax.ppermute(dkv_other, "ctx", X_SWAP).astype(F32)
    dq = dq_keep[0] + dq_got[0] + dq_x
    dkv = dkv_own[0] + dkv_got[0] + dkv_x
    grads = jnp.concatenate([dq, dkv], axis=1).astype(BF16)
    moved = lax.ppermute(after(turned_tp, dkv_send), ("ctx", "tp"), TURN_Z)
    grads_all = lax.all_gather(grads, "ctx", axis=0, tiled=True, axis_index_groups=Z_GROUPS)

    moved_x = lax.ppermute(moved, "tp", TP_X)
    pair = jnp.concatenate([moved, moved_x], axis=0)
    n_up = lax.ppermute(pair, "tp", TP_UP)
    n_down = lax.ppermute(pair, "tp", TP_DOWN)
    turned = call(
        normed_kernel,
        shaped((640, PLANES * ROWS), BF16),
        place,
        pair,
        n_up,
        n_down,
        lax.ppermute(n_up[:ROWS], "tp", TP_UP),
        lax.ppermute(n_down[ROWS:], "tp", TP_DOWN),
        smem=1,
        name="normed_columns",
    )
    sums = call(
        product_kernel,
        (shaped((2, 160, W), F32), shaped((2, 160, W), BF16)) * 3,
        place,
        turned,
        grads_all,
        smem=1,
        flops=2 * 640 * 1024 * 3 * W,
        name="weight_product",
    )
    return tuple(row_sum(sums[2 * i], sums[2 * i + 1], xl).astype(BF16) for i in range(3))


def solution(mesh):
    return jax.shard_map(
        shards,
        mesh=mesh,
        in_specs=(
            P("ctx", "tp"),
            P("ctx", "tp"),
            P("ctx", "tp"),
            P("ctx", "tp"),
            P("ctx", "tp"),
            P(),
        ),
        out_specs=(P("ctx", "tp"), P("ctx", "tp"), P("ctx", "tp")),
        check_vma=False,
    )
```
